32 devices in a mesh: wide: 8 (over y, x, core), narrow: 4 (over z).
Axes of the slice: x: 2, y: 2, z: 4, core: 2. Of those that a mesh axis runs over, the one named last changes fastest.
Arguments:
- state: float32 [4, 64, 64, 2048], P(None, 'narrow', None, 'wide'), may hold values from -6 to 6
- stiffness: float32 [64, 64, 2048], P('narrow', None, 'wide'), may hold values from 0.5 to 1.5
- liner_cells: int32 [4, 8, 8, 128], P('narrow', 'wide'), may hold values from 0 to 262143, as said below
- neighbour_cells: int32 [4, 8, 8, 128], P('narrow', 'wide'), may hold values from 0 to 262143, as said below
- send_counts: int32 [4, 8, 8], P('narrow', 'wide'), may hold values from 1 to 128, as said below
- history: float32 [4, 8, 8, 128, 512], P('narrow', 'wide'), may hold values from -6 to 6
- slot_panel: int32 [4, 8, 8, 128], P('narrow', 'wide'), may hold values from 0 to 3
- kernels: float32 [32, 512], P('wide'), may hold values from -0.25 to 0.25
- conductance: float32 [32], P('wide'), may hold values from 0.2 to 1
Outputs:
- state_out: float32 [4, 64, 64, 2048], P(None, 'narrow', None, 'wide')
The draws below stay inside these ranges and needn't reach their ends.
Inputs may be any that keep to these rules, and one draw needn't show every extreme that they name: `liner_cells`: A cell of tile (j, w) in its own numbering (r * 64 + z) * 256 + t with 1 <= z <= 62; slots beyond the live count hold such cells too and carry nothing. `neighbour_cells`: the cell one axial plane beside the slot's cell, same r and t. `send_counts`: for every radial index j one owner receives exactly 128 live slots from every tile.
All inputs are finite; a program needn't handle non-finite values.
Results may differ from the reference program's by a relative error of at most 0.0003.
Values sent between devices are 32-bit elements; how exact they have to be, the bound alone decides.
A program may use at most 64 MiB of HBM per device.

```python
import math
import jax
import jax.numpy as jnp
from jax import lax

CR = 16
CT = 256
PLANES = 64
CAP = 128
PAN_DEV = 4
TAPS = 512
ITERS = 4
NR = 64
NT = 2048
PANELS = 32
N_WIDE = 8
N_NARROW = 4


def liner_pair(key):
    shape = (N_NARROW, N_WIDE, N_WIDE, CAP)
    keys = jax.random.split(jax.random.fold_in(key, 11), 4)
    radial_at = jax.random.randint(keys[0], shape, 0, CR, dtype=jnp.int32)
    plane_at = jax.random.randint(keys[1], shape, 1, PLANES - 1, dtype=jnp.int32)
    around_at = jax.random.randint(keys[2], shape, 0, CT, dtype=jnp.int32)
    side = 2 * jax.random.randint(keys[3], shape, 0, 2, dtype=jnp.int32) - 1
    cells = (radial_at * PLANES + plane_at) * CT + around_at
    beside = (radial_at * PLANES + plane_at + side) * CT + around_at
    return (cells, beside)


def draw_liner_cells(key, part):
    return liner_pair(key)[0]


def draw_neighbour_cells(key, part):
    return liner_pair(key)[1]


def draw_send_counts(key, part):
    shape = (N_NARROW, N_WIDE, N_WIDE)
    keys = jax.random.split(jax.random.fold_in(key, 23), 2)
    fullest = jax.random.randint(keys[0], (N_NARROW,), 0, N_WIDE, dtype=jnp.int32)
    base = jax.random.randint(keys[1], shape, CAP // 4, CAP + 1, dtype=jnp.int32)
    owner = lax.broadcasted_iota(jnp.int32, shape, 2)
    return jnp.where(owner == fullest[:, None, None], CAP, base).astype(jnp.int32)


def with_ends(entries, own_key, least, high):
    longest = entries.shape.index(max(entries.shape))
    spots = []
    for shift in (0, 1):
        where = [jax.random.randint(jax.random.fold_in(own_key, axis), (), 0, length) for axis, length in enumerate(entries.shape)]
        where[longest] = (where[longest] + shift) % entries.shape[longest]
        spots.append(tuple(where))
    return entries.at[spots[0]].set(least).at[spots[1]].set(high)


def block_levels(stream_key, dims, pieces, low, top_value):
    def one(dim, shards_of):
        steps = jax.random.uniform(jax.random.fold_in(jax.random.fold_in(stream_key, 6), dim), (shards_of,), jnp.float32, low / len(pieces), top_value / len(pieces))
        return jnp.repeat(jnp.exp(steps), dims[dim] // shards_of).reshape((-1,) + (1,) * (len(dims) - dim - 1))

    loudness = one(*pieces[0])
    for cut in pieces[1:]:
        loudness = loudness * one(*cut)
    return loudness


def scatter_about(key, dims, deviation, most, cuts=(), kind=jnp.bfloat16):
    array = jax.random.normal(key, dims, jnp.float32) * deviation
    if len(cuts) > 0:
        array = block_levels(key, dims, cuts, -0.22, 0.18) * array
    return jnp.clip(array, min=-most, max=most).astype(kind)


def setup_inputs(seed: int = 0) -> dict:
    key_list = jax.random.split(jax.random.key(seed), 10)
    state = scatter_about(key_list[0], (4, NR, PLANES, NT), 1.0, 6.0, ((1, 4), (3, 8)), jnp.float32)
    stiffness = jnp.clip(jnp.exp(math.log(1.5) - 1.0986123 * jax.random.uniform(key_list[1], (NR, PLANES, NT), jnp.float32) ** block_levels(key_list[1], (NR, PLANES, NT), ((0, 4), (2, 8)), -0.2, 0.2)), 0.5, 1.5)
    liner_cells = draw_liner_cells(jax.random.fold_in(key_list[9], 71), 0)
    neighbour_cells = draw_neighbour_cells(jax.random.fold_in(key_list[9], 71), 0)
    send_counts = draw_send_counts(jax.random.fold_in(key_list[9], 71), 0)
    history = scatter_about(key_list[5], (N_NARROW, N_WIDE, N_WIDE, CAP, TAPS), 1.0, 6.0, ((0, 4), (1, 8)), jnp.float32)
    slot_panel = with_ends(jax.random.randint(key_list[6], (N_NARROW, N_WIDE, N_WIDE, CAP), 0, PAN_DEV), jax.random.fold_in(key_list[6], 1), 0, PAN_DEV - 1).astype(jnp.int32)
    kernels = scatter_about(key_list[7], (PANELS, TAPS), TAPS ** -0.5, 0.25, ((0, 8),), jnp.float32)
    conductance = jnp.clip(jnp.exp(math.log(1.0) - 1.609438 * jax.random.uniform(key_list[8], (PANELS,), jnp.float32) ** block_levels(key_list[8], (PANELS,), ((0, 8),), -0.2, 0.2)), 0.2, 1.0)
    return dict(state=state, stiffness=stiffness, liner_cells=liner_cells, neighbour_cells=neighbour_cells, send_counts=send_counts, history=history, slot_panel=slot_panel, kernels=kernels, conductance=conductance)


time_step = 0.5
keep_share = 0.6
far_share = 0.4


def central(ext, axis):
    count = ext.shape[axis] - 6

    def offset(shift):
        return lax.slice_in_dim(ext, 3 + shift, 3 + shift + count, axis=axis)

    return (45.0 * (offset(1) - offset(-1)) - 9.0 * (offset(2) - offset(-2)) + (offset(3) - offset(-3))) / 60.0


def pad_radial(field):
    return jnp.pad(field, ((3, 3), (0, 0), (0, 0)))


def pad_planes(field):
    return jnp.pad(field, ((0, 0), (3, 3), (0, 0)))


def wrap_around(field):
    return jnp.concatenate([field[:, :, -3:], field, field[:, :, :3]], axis=2)


def reference(state, stiffness, liner_cells, neighbour_cells, send_counts, history, slot_panel, kernels, conductance):
    pressure, radial, axial, beside_all = state[0], state[1], state[2], state[3]
    kern = kernels.reshape(N_WIDE, PAN_DEV, TAPS)
    flipped = kern[:, :, ::-1]
    columns = []
    for lag in range(ITERS):
        columns.append(jnp.concatenate([jnp.zeros((N_WIDE, PAN_DEV, lag), jnp.float32), flipped[:, :, :TAPS - lag]], axis=2))
    toeplitz = jnp.stack(columns, axis=3)
    full = jnp.einsum('jowct,oqtn->jowqnc', history, toeplitz, precision=lax.Precision.HIGHEST, preferred_element_type=jnp.float32)
    choose = lax.broadcasted_iota(jnp.int32, (1, 1, 1, PAN_DEV, 1), 3)
    onehot = (slot_panel[:, :, :, None, :] == choose).astype(jnp.float32)
    responses = jnp.sum(onehot[:, :, :, :, None, :] * full, axis=3)
    khead = jnp.sum(onehot[:, :, :, :, None, :] * kern[None, :, None, :, :ITERS - 1, None], axis=3)
    admit = jnp.sum(onehot * conductance.reshape(N_WIDE, PAN_DEV)[None, :, None, :, None], axis=3)
    shape = liner_cells.shape
    row_j = lax.broadcasted_iota(jnp.int32, shape, 0)
    tile_w = lax.broadcasted_iota(jnp.int32, shape, 1)

    def global_index(cells):
        radial_at = cells // (PLANES * CT)
        plane_at = (cells // CT) % PLANES
        around_at = cells % CT
        return ((row_j * CR + radial_at) * PLANES + plane_at) * NT + tile_w * CT + around_at

    cell_index = global_index(liner_cells).reshape(-1)
    side_index = global_index(neighbour_cells).reshape(-1)
    live = (lax.broadcasted_iota(jnp.int32, shape, 3) < send_counts[:, :, :, None]).astype(jnp.float32)
    previous = []
    for current in range(ITERS):
        wall = pressure.reshape(-1)[cell_index].reshape(shape)
        arrived = jnp.transpose(wall, (0, 2, 1, 3))
        velocity = admit * arrived + responses[:, :, :, current, :]
        for back_step in range(1, current + 1):
            velocity = velocity + khead[:, :, :, back_step - 1, :] * previous[current - back_step]
        previous.append(arrived)
        returned = jnp.transpose(velocity, (0, 2, 1, 3))
        radial = radial - time_step * central(pad_radial(pressure), 0)
        axial = axial - time_step * central(pad_planes(pressure), 1)
        beside_all = beside_all - time_step * central(wrap_around(pressure), 2)
        spread = central(pad_radial(radial), 0) + central(pad_planes(axial), 1) + central(wrap_around(beside_all), 2)
        pressure = pressure - time_step * stiffness * spread
        flux = time_step * returned * live
        flat = pressure.reshape(-1).at[cell_index].add(-(keep_share * flux).reshape(-1))
        flat = flat.at[side_index].add(-(far_share * flux).reshape(-1))
        pressure = flat.reshape(pressure.shape)
    return jnp.stack([pressure, radial, axial, beside_all])
```

```python
import functools

import jax
import jax.numpy as jnp
from jax import lax
from jax.experimental import pallas as pl
from jax.experimental.pallas import tpu as pltpu
from jax.sharding import PartitionSpec as P

ITERS = 4
WIDE_HALO = 6
THIN_HALO = 3
STEP = 0.5 / 60.0
MESH = pl.DeviceIdType.MESH
F32 = jnp.float32
BF16 = jnp.bfloat16


def split(values):
    high = values.astype(BF16)
    return high, (values - high.astype(F32)).astype(BF16)


def dot(a, b):
    return jnp.dot(a, b, preferred_element_type=F32)


def band(offset):
    value = jnp.where(jnp.abs(offset) == 1, 45.0, 0.0)
    value = jnp.where(jnp.abs(offset) == 2, -9.0, value)
    value = jnp.where(jnp.abs(offset) == 3, 1.0, value)
    return jnp.where(offset < 0, -value, value)


def iota(shape, dim):
    return lax.broadcasted_iota(jnp.int32, shape, dim)


def kernel(
    n_wide,
    n_narrow,
    state,
    stiff_in,
    cells_ref,
    beside_ref,
    counts_ref,
    history_in,
    panel_ref,
    kernels_ref,
    conduct_ref,
    out,
    stiff,
    history,
    halo,
    thin,
    edge_send,
    edge_recv,
    around_side,
    pick,
    spread,
    column,
    x_high,
    x_low,
    w_high,
    w_low,
    base,
    bands,
    blocks,
    answer_send,
    answer_recv,
    stage,
    coefs,
    walls,
    toeplitz,
    constants,
    load_sem,
    radial_send,
    radial_recv,
    thin_send,
    thin_recv,
    edge_send_sem,
    edge_recv_sem,
    answer_send_sem,
    answer_recv_sem,
):
    wide = lax.axis_index("wide")
    narrow = lax.axis_index("narrow")
    layers, planes, around = out.shape[1:]
    rows = layers * planes
    slots = panel_ref.shape[1]
    panels, taps = kernels_ref.shape
    left, right = lax.rem(wide + n_wide - 1, n_wide), lax.rem(wide + 1, n_wide)
    has_low, has_high = narrow > 0, narrow < n_narrow - 1

    loads = [
        pltpu.make_async_copy(state.at[k], out.at[k], load_sem.at[k]) for k in range(4)
    ]
    loads.append(pltpu.make_async_copy(history_in, history, load_sem.at[4]))
    loads.append(pltpu.make_async_copy(stiff_in, stiff, load_sem.at[5]))
    for which in (0, 3, 4, 1, 2, 5):
        loads[which].start()

    barrier = pltpu.get_barrier_semaphore()
    for k in range(1, n_wide):
        peer = lax.rem(wide + k, n_wide)
        pl.semaphore_signal(barrier, inc=1, device_id={"wide": peer}, device_id_type=MESH)

    @pl.when(has_low)
    def _():
        pl.semaphore_signal(
            barrier, inc=1, device_id={"narrow": narrow - 1}, device_id_type=MESH
        )

    @pl.when(has_high)
    def _():
        pl.semaphore_signal(
            barrier, inc=1, device_id={"narrow": narrow + 1}, device_id_type=MESH
        )

    @pl.when(jnp.logical_not(has_low))
    def _():
        halo[:, 0] = jnp.zeros(halo.shape[:1] + halo.shape[2:], F32)
        thin[0] = jnp.zeros(thin.shape[1:], F32)

    @pl.when(jnp.logical_not(has_high))
    def _():
        halo[:, 1] = jnp.zeros(halo.shape[:1] + halo.shape[2:], F32)
        thin[1] = jnp.zeros(thin.shape[1:], F32)

    beside = jnp.where(has_low, 1, 0) + jnp.where(has_high, 1, 0)
    pl.semaphore_wait(barrier, n_wide - 1 + beside)

    def radial_copy(source, step, side, peer=None):
        if peer is None:
            peer = narrow - 1 if side == 0 else narrow + 1
        first = 0 if side == 0 else layers - WIDE_HALO
        return pltpu.make_async_remote_copy(
            src_ref=source.at[0, pl.ds(first, WIDE_HALO)],
            dst_ref=halo.at[step, 1 - side],
            send_sem=radial_send.at[step, side],
            recv_sem=radial_recv.at[step, 1 - side],
            device_id={"narrow": peer},
            device_id_type=MESH,
        )

    def thin_copy(side, peer=None):
        if peer is None:
            peer = narrow - 1 if side == 0 else narrow + 1
        first = 0 if side == 0 else layers - THIN_HALO
        return pltpu.make_async_remote_copy(
            src_ref=state.at[1, pl.ds(first, THIN_HALO)],
            dst_ref=thin.at[1 - side],
            send_sem=thin_send.at[side],
            recv_sem=thin_recv.at[1 - side],
            device_id={"narrow": peer},
            device_id_type=MESH,
        )

    def radial_arrival(step, side):
        return radial_copy(out, step, 1 - side, narrow - 1 if side == 0 else narrow + 1)

    def thin_arrival(side):
        return thin_copy(1 - side, narrow - 1 if side == 0 else narrow + 1)

    def edge_copy(slot, side):
        return pltpu.make_async_remote_copy(
            src_ref=edge_send.at[slot, side],
            dst_ref=edge_recv.at[slot, 1 - side],
            send_sem=edge_send_sem.at[slot, side],
            recv_sem=edge_recv_sem.at[slot, 1 - side],
            device_id={"wide": left if side == 0 else right},
            device_id_type=MESH,
        )

    sides = ((0, has_low), (1, has_high))
    for side, there in sides:

        @pl.when(there)
        def _(side=side):
            radial_copy(state, 0, side).start()
            thin_copy(side).start()

    lane = iota((planes, 128), 1)

    def pack(field, slot):
        low = jnp.zeros((planes, 128), F32)
        high = jnp.zeros((planes, 128), F32)
        for r in range(layers):
            here = (lane >= 8 * r) & (lane < 8 * r + 8)
            first = out[field, r, :, 0:128]
            last = out[field, r, :, around - 128 : around]
            low = jnp.where(here, pltpu.roll(first, 8 * r, 1) if r else first, low)
            high = jnp.where(here, pltpu.roll(last, (8 * r + 8) % 128, 1), high)
        edge_send[slot, 0] = low
        edge_send[slot, 1] = high
        edge_copy(slot, 0).start()
        edge_copy(slot, 1).start()

    def unpack(slot, r):
        low = edge_recv[slot, 1]
        high = edge_recv[slot, 0]
        low = pltpu.roll(low, (128 - 8 * r) % 128, 1) if r else low
        turn = (120 - 8 * r) % 128
        high = pltpu.roll(high, turn, 1) if turn else high
        return jnp.where(lane < 8, low, jnp.where(lane >= 120, high, 0.0))

    def set_split(r):
        high, low = split(out[0, r])
        x_high[r, :, 0:around] = high
        x_low[r, :, 0:around] = low

    loads[0].wait()
    pack(0, 0)
    loads[3].wait()
    pack(3, ITERS)
    for r in range(layers):
        set_split(r)

    turned = jnp.where(iota((taps, taps), 0) + iota((taps, taps), 1) == taps - 1, 1.0, 0.0)
    backward = jnp.dot(
        kernels_ref[...], turned, precision=lax.Precision.HIGHEST, preferred_element_type=F32
    )
    toeplitz[...] = jnp.zeros_like(toeplitz)
    constants[...] = jnp.zeros_like(constants)
    late = iota((1, taps), 1)
    for q in range(panels):
        row = backward[q : q + 1]
        for lag in range(ITERS):
            shifted = pltpu.roll(row, lag, 1) if lag else row
            toeplitz[8 * q + lag : 8 * q + lag + 1] = jnp.where(late >= lag, shifted, 0.0)
        constants[8 * q + 4 : 8 * q + 5] = jnp.full((1, slots), conduct_ref[q], F32)
        for k in range(ITERS - 1):
            constants[8 * q + 5 + k : 8 * q + 6 + k] = jnp.broadcast_to(
                kernels_ref[q : q + 1, k : k + 1], (1, slots)
            )
    loads[4].wait()
    ours = iota((8 * panels, slots), 0) >> 3

    @pl.loop(0, n_wide)
    def _(o):
        full = lax.dot_general(
            toeplitz[...],
            history[pl.ds(pl.multiple_of(o * slots, slots), slots)],
            (((1,), (1,)), ((), ())),
            precision=lax.Precision.HIGHEST,
            preferred_element_type=F32,
        )
        chosen = panel_ref[pl.ds(o, 1)] == ours
        terms = jnp.where(chosen, full + constants[...], 0.0)
        answer_send[o] = jnp.sum(terms.reshape(panels, 8, slots), axis=0)

    def answer_copy(k):
        peer = lax.rem(wide + k, n_wide)
        return pltpu.make_async_remote_copy(
            src_ref=answer_send.at[peer],
            dst_ref=answer_recv.at[wide],
            send_sem=answer_send_sem.at[k],
            recv_sem=answer_recv_sem.at[k],
            device_id={"wide": peer},
            device_id_type=MESH,
        )

    for k in range(1, n_wide):
        answer_copy(k).start()
    answer_recv[wide] = answer_send[wide]

    ring = around + 128
    gap = iota((ring, ring), 0) - iota((ring, ring), 1)
    gap = jnp.where(gap > ring // 2, gap - ring, jnp.where(gap < -(ring // 2), gap + ring, gap))
    bands[...] = band(gap).astype(BF16)
    size = blocks.shape[0]
    at_row, at_col = iota((size, size), 0), iota((size, size), 1)
    blocks[...] = jnp.where(
        (at_row // planes) == (at_col // planes), band(at_col - at_row), 0.0
    ).astype(BF16)

    shift = around.bit_length() - 1
    cells = cells_ref[...]
    own_row = cells >> shift
    side_row = beside_ref[...] >> shift
    stage[...] = jnp.zeros_like(stage)
    stage[0:n_wide] = own_row.astype(F32)
    stage[n_wide : 2 * n_wide] = (cells & (around - 1)).astype(F32)
    upright = jnp.transpose(stage[...])
    place = iota((slots, rows), 1).astype(F32)
    where = iota((slots, around), 1).astype(F32)
    level = iota((rows, slots), 0)
    for o in range(n_wide):
        span = slice(o * slots, (o + 1) * slots)
        pick[span] = jnp.where(place == upright[:, o : o + 1], 1.0, 0.0).astype(BF16)
        column[span] = jnp.where(
            where == upright[:, n_wide + o : n_wide + o + 1], 1.0, 0.0
        )
        spread[:, span] = (
            jnp.where(level == own_row[o : o + 1], 3.0, 0.0)
            + jnp.where(level == side_row[o : o + 1], 2.0, 0.0)
        ).astype(BF16)

    walls[...] = jnp.zeros_like(walls)
    live = jnp.where(iota((slots, n_wide), 0) < counts_ref[...], 1.0, 0.0)

    for k in range(1, n_wide):
        answer_copy(k).wait_recv()
    for o in range(n_wide):
        for m in range(8):
            stage[m * n_wide + o : m * n_wide + o + 1] = answer_recv[o, m : m + 1]
    upright = jnp.transpose(stage[...])
    for m in range(8):
        coefs[m] = upright[:, m * n_wide : (m + 1) * n_wide]

    edge_copy(ITERS, 0).wait_recv()
    edge_copy(ITERS, 1).wait_recv()
    for r in range(layers):
        around_side[r] = unpack(ITERS, r)
    for which in (1, 2, 5):
        loads[which].wait()

    group = size // planes
    fan = 4

    def pressure_at(step, r):
        if r < 0:
            return halo[step, 0, r + WIDE_HALO]
        if r >= layers:
            return halo[step, 1, r - layers]
        return out[0, r]

    def radial_at(r):
        if r < 0:
            return thin[0, r + THIN_HALO]
        if r >= layers:
            return thin[1, r - layers]
        return out[1, r]

    def differ(get, r):
        return (
            45.0 * (get(r + 1) - get(r - 1))
            - 9.0 * (get(r + 2) - get(r - 2))
            + (get(r + 3) - get(r - 3))
        )

    @pl.loop(0, ITERS)
    def _(step):
        for first in range(0, n_wide, fan):
            span = slice(first * slots, (first + fan) * slots)
            low = pick[span]
            found = dot(low, x_high[:, :, 0:around].reshape(rows, around)) + dot(
                low, x_low[:, :, 0:around].reshape(rows, around)
            )
            wall = jnp.sum(found * column[span], axis=1, keepdims=True)
            for o in range(fan):
                walls[0, :, first + o : first + o + 1] = wall[o * slots : (o + 1) * slots]
        wall = walls[0]
        velocity = coefs[4] * wall + coefs[step]
        for k in range(1, ITERS):
            velocity = velocity + coefs[4 + k] * walls[k]
        for k in range(ITERS - 1, 0, -1):
            walls[k] = walls[k - 1]
        flux = velocity * live
        for o in range(n_wide):
            span = slice(o * slots, (o + 1) * slots)
            high, low = split(flux[:, o : o + 1] * column[span])
            w_high[span] = high
            w_low[span] = low

        edge_copy(step, 0).wait_recv()
        edge_copy(step, 1).wait_recv()
        for r in range(layers):
            high, low = split(unpack(step, r))
            x_high[r, :, around:ring] = high
            x_low[r, :, around:ring] = low

        @pl.loop(0, layers // group)
        def _(chunk):
            part = pl.ds(chunk * group, group)
            span = pl.ds(pl.multiple_of(chunk * size, size), size)

            def flat(ref, width):
                return ref.reshape(size, width)

            high, low = flat(x_high[part], ring), flat(x_low[part], ring)
            along = dot(blocks[...], high[:, :around]) + dot(blocks[...], low[:, :around])
            axial = flat(out[2, part], around) - STEP * along
            out[2, part] = axial.reshape(group, planes, around)
            turn = dot(high, bands[...]) + dot(low, bands[...])
            inner = flat(out[3, part], around) - STEP * turn[:, :around]
            outer = flat(around_side[part], 128) - STEP * turn[:, around:]
            out[3, part] = inner.reshape(group, planes, around)
            around_side[part] = outer.reshape(group, planes, 128)
            high, low = split(axial)
            total = dot(blocks[...], high) + dot(blocks[...], low)
            for block, at in ((inner, slice(0, around)), (outer, slice(around, ring))):
                high, low = split(block)
                kept = bands[at, :around]
                total = total + (dot(high, kept) + dot(low, kept))
            added = dot(spread[span], w_high[...]) + dot(spread[span], w_low[...])
            base[part] = (
                flat(out[0, part], around)
                - (STEP * flat(stiff[part], around)) * total
                - 0.1 * added
            ).reshape(group, planes, around)

        get = functools.partial(pressure_at, step)
        for r in range(THIN_HALO, layers - THIN_HALO):
            out[1, r] = out[1, r] - STEP * differ(get, r)
        for side, there in sides:

            @pl.when(there)
            def _(side=side):
                radial_arrival(step, side).wait_recv()

                @pl.when(step == 0)
                def _():
                    thin_arrival(side).wait_recv()

        for r in range(THIN_HALO):
            out[1, r] = out[1, r] - STEP * differ(get, r)
            top = layers - 1 - r
            out[1, top] = out[1, top] - STEP * differ(get, top)
        for side, there in sides:

            @pl.when(there)
            def _(side=side):
                for k in range(THIN_HALO):
                    r = k - THIN_HALO if side == 0 else layers + k
                    thin[side, k] = thin[side, k] - STEP * differ(get, r)

                radial_copy(out, step, side).wait_send()

        def renew(r):
            out[0, r] = base[r] - (STEP * stiff[r]) * differ(radial_at, r)

        for r in range(WIDE_HALO):
            renew(r)

        @pl.when((step < ITERS - 1) & has_low)
        def _():
            radial_copy(out, step + 1, 0).start()

        for r in range(layers - WIDE_HALO, layers):
            renew(r)

        @pl.when((step < ITERS - 1) & has_high)
        def _():
            radial_copy(out, step + 1, 1).start()

        for r in range(WIDE_HALO, layers - WIDE_HALO):
            renew(r)

        @pl.when(step < ITERS - 1)
        def _():
            pack(0, step + 1)
            for r in range(layers):
                set_split(r)

    for side, there in sides:

        @pl.when(there)
        def _(side=side):
            thin_copy(side).wait_send()

    for slot in range(ITERS + 1):
        edge_copy(slot, 0).wait_send()
        edge_copy(slot, 1).wait_send()
    for k in range(1, n_wide):
        answer_copy(k).wait_send()


def shards(n_wide, n_narrow, *arrays):
    (state, stiffness, cells, besides, counts, history, panel, kernels, conductance) = arrays
    _, layers, planes, around = state.shape
    peers, slots = cells.shape[2:]
    taps = kernels.shape[1]
    panels = kernels.shape[0]
    rows, count, ring = layers * planes, peers * slots, around + 128
    group = max(1, min(layers, 256 // planes))
    any_space = pl.BlockSpec(memory_space=pl.ANY)
    vmem = pl.BlockSpec(memory_space=pltpu.VMEM)
    dma = pltpu.SemaphoreType.DMA
    scratch = [
        pltpu.VMEM((layers, planes, around), F32),
        pltpu.VMEM((count, taps), F32),
        pltpu.VMEM((ITERS, 2, WIDE_HALO, planes, around), F32),
        pltpu.VMEM((2, THIN_HALO, planes, around), F32),
        pltpu.VMEM((ITERS + 1, 2, planes, 128), F32),
        pltpu.VMEM((ITERS + 1, 2, planes, 128), F32),
        pltpu.VMEM((layers, planes, 128), F32),
        pltpu.VMEM((count, rows), BF16),
        pltpu.VMEM((rows, count), BF16),
        pltpu.VMEM((count, around), F32),
        pltpu.VMEM((layers, planes, ring), BF16),
        pltpu.VMEM((layers, planes, ring), BF16),
        pltpu.VMEM((count, around), BF16),
        pltpu.VMEM((count, around), BF16),
        pltpu.VMEM((layers, planes, around), F32),
        pltpu.VMEM((ring, ring), BF16),
        pltpu.VMEM((group * planes, group * planes), BF16),
        pltpu.VMEM((peers, 8, slots), F32),
        pltpu.VMEM((peers, 8, slots), F32),
        pltpu.VMEM((max(128, 8 * peers), slots), F32),
        pltpu.VMEM((8, slots, peers), F32),
        pltpu.VMEM((ITERS, slots, peers), F32),
        pltpu.VMEM((8 * panels, taps), F32),
        pltpu.VMEM((8 * panels, slots), F32),
        dma((6,)),
        dma((ITERS, 2)),
        dma((ITERS, 2)),
        dma((2,)),
        dma((2,)),
        dma((ITERS + 1, 2)),
        dma((ITERS + 1, 2)),
        dma((peers,)),
        dma((peers,)),
    ]
    return pl.pallas_call(
        functools.partial(kernel, n_wide, n_narrow),
        out_shape=jax.ShapeDtypeStruct(state.shape, F32),
        in_specs=[any_space, any_space, vmem, vmem, vmem, any_space, vmem, vmem]
        + [pl.BlockSpec(memory_space=pltpu.SMEM)],
        out_specs=vmem,
        scratch_shapes=scratch,
        compiler_params=pltpu.CompilerParams(
            collective_id=0, has_side_effects=True, vmem_limit_bytes=56 * 1024 * 1024
        ),
    )(
        state,
        stiffness,
        cells.reshape(peers, slots),
        besides.reshape(peers, slots),
        counts.reshape(1, peers),
        history.reshape(count, taps),
        panel.reshape(peers, slots),
        kernels,
        conductance,
    )


def solution(mesh):
    return jax.shard_map(
        functools.partial(shards, mesh.shape["wide"], mesh.shape["narrow"]),
        mesh=mesh,
        in_specs=(
            P(None, "narrow", None, "wide"),
            P("narrow", None, "wide"),
            P("narrow", "wide", None, None),
            P("narrow", "wide", None, None),
            P("narrow", "wide", None),
            P("narrow", "wide", None, None, None),
            P("narrow", "wide", None, None),
            P("wide", None),
            P("wide"),
        ),
        out_specs=P(None, "narrow", None, "wide"),
        check_vma=False,
    )
```

```python
import functools

import jax
import jax.numpy as jnp
from jax import lax
from jax.experimental import pallas as pl
from jax.experimental.pallas import tpu as pltpu
from jax.sharding import PartitionSpec as P

ITERS = 4
WIDE_HALO = 6
THIN_HALO = 3
STEP = 0.5 / 60.0
MESH = pl.DeviceIdType.MESH
F32 = jnp.float32
BF16 = jnp.bfloat16


def split(values):
    high = values.astype(BF16)
    return high, (values - high.astype(F32)).astype(BF16)


def dot(a, b):
    return jnp.dot(a, b, preferred_element_type=F32)


def band(offset):
    value = jnp.where(jnp.abs(offset) == 1, 45.0, 0.0)
    value = jnp.where(jnp.abs(offset) == 2, -9.0, value)
    value = jnp.where(jnp.abs(offset) == 3, 1.0, value)
    return jnp.where(offset < 0, -value, value)


def iota(shape, dim):
    return lax.broadcasted_iota(jnp.int32, shape, dim)


def kernel(
    n_wide,
    n_narrow,
    state,
    stiff_in,
    cells_in,
    beside_in,
    counts_in,
    history_in,
    panel_in,
    kernels_in,
    conduct_ref,
    out,
    cells_ref,
    beside_ref,
    counts_ref,
    panel_ref,
    kernels_ref,
    stiff,
    history,
    halo,
    thin,
    edge_send,
    edge_recv,
    around_side,
    pick,
    spread,
    column,
    x_high,
    x_low,
    w_high,
    w_low,
    base,
    bands,
    blocks,
    answer_send,
    answer_recv,
    stage,
    coefs,
    walls,
    toeplitz,
    constants,
    load_sem,
    radial_send,
    radial_recv,
    thin_send,
    thin_recv,
    edge_send_sem,
    edge_recv_sem,
    answer_send_sem,
    answer_recv_sem,
):
    wide = lax.axis_index("wide")
    narrow = lax.axis_index("narrow")
    layers, planes, around = out.shape[1:]
    rows = layers * planes
    slots = panel_in.shape[1]
    panels, taps = kernels_in.shape
    left, right = lax.rem(wide + n_wide - 1, n_wide), lax.rem(wide + 1, n_wide)
    has_low, has_high = narrow > 0, narrow < n_narrow - 1

    loads = [
        pltpu.make_async_copy(state.at[k], out.at[k], load_sem.at[k]) for k in range(4)
    ]
    loads.append(pltpu.make_async_copy(history_in, history, load_sem.at[4]))
    loads.append(pltpu.make_async_copy(stiff_in, stiff, load_sem.at[5]))
    small = (
        (cells_in, cells_ref),
        (beside_in, beside_ref),
        (counts_in, counts_ref),
        (panel_in, panel_ref),
        (kernels_in, kernels_ref),
    )
    for k, (source, target) in enumerate(small):
        loads.append(pltpu.make_async_copy(source, target, load_sem.at[6 + k]))
    for which in (6, 7, 8, 9, 10, 0, 4, 3, 1, 2, 5):
        loads[which].start()

    barrier = pltpu.get_barrier_semaphore()
    for k in range(1, n_wide):
        peer = lax.rem(wide + k, n_wide)
        pl.semaphore_signal(barrier, inc=1, device_id={"wide": peer}, device_id_type=MESH)

    @pl.when(has_low)
    def _():
        pl.semaphore_signal(
            barrier, inc=1, device_id={"narrow": narrow - 1}, device_id_type=MESH
        )

    @pl.when(has_high)
    def _():
        pl.semaphore_signal(
            barrier, inc=1, device_id={"narrow": narrow + 1}, device_id_type=MESH
        )

    @pl.when(jnp.logical_not(has_low))
    def _():
        halo[:, 0] = jnp.zeros(halo.shape[:1] + halo.shape[2:], F32)
        thin[0] = jnp.zeros(thin.shape[1:], F32)

    @pl.when(jnp.logical_not(has_high))
    def _():
        halo[:, 1] = jnp.zeros(halo.shape[:1] + halo.shape[2:], F32)
        thin[1] = jnp.zeros(thin.shape[1:], F32)

    beside = jnp.where(has_low, 1, 0) + jnp.where(has_high, 1, 0)
    pl.semaphore_wait(barrier, n_wide - 1 + beside)

    def radial_copy(source, step, side, peer=None):
        if peer is None:
            peer = narrow - 1 if side == 0 else narrow + 1
        first = 0 if side == 0 else layers - WIDE_HALO
        return pltpu.make_async_remote_copy(
            src_ref=source.at[0, pl.ds(first, WIDE_HALO)],
            dst_ref=halo.at[step, 1 - side],
            send_sem=radial_send.at[step, side],
            recv_sem=radial_recv.at[step, 1 - side],
            device_id={"narrow": peer},
            device_id_type=MESH,
        )

    def thin_copy(side, peer=None):
        if peer is None:
            peer = narrow - 1 if side == 0 else narrow + 1
        first = 0 if side == 0 else layers - THIN_HALO
        return pltpu.make_async_remote_copy(
            src_ref=state.at[1, pl.ds(first, THIN_HALO)],
            dst_ref=thin.at[1 - side],
            send_sem=thin_send.at[side],
            recv_sem=thin_recv.at[1 - side],
            device_id={"narrow": peer},
            device_id_type=MESH,
        )

    def radial_arrival(step, side):
        return radial_copy(out, step, 1 - side, narrow - 1 if side == 0 else narrow + 1)

    def thin_arrival(side):
        return thin_copy(1 - side, narrow - 1 if side == 0 else narrow + 1)

    def edge_copy(slot, side):
        return pltpu.make_async_remote_copy(
            src_ref=edge_send.at[slot, side],
            dst_ref=edge_recv.at[slot, 1 - side],
            send_sem=edge_send_sem.at[slot, side],
            recv_sem=edge_recv_sem.at[slot, 1 - side],
            device_id={"wide": left if side == 0 else right},
            device_id_type=MESH,
        )

    sides = ((0, has_low), (1, has_high))
    for side, there in sides:

        @pl.when(there)
        def _(side=side):
            radial_copy(state, 0, side).start()
            thin_copy(side).start()

    lane = iota((planes, 128), 1)

    def pack(field, slot):
        low = jnp.zeros((planes, 128), F32)
        high = jnp.zeros((planes, 128), F32)
        for r in range(layers):
            here = (lane >= 8 * r) & (lane < 8 * r + 8)
            first = out[field, r, :, 0:128]
            last = out[field, r, :, around - 128 : around]
            low = jnp.where(here, pltpu.roll(first, 8 * r, 1) if r else first, low)
            high = jnp.where(here, pltpu.roll(last, (8 * r + 8) % 128, 1), high)
        edge_send[slot, 0] = low
        edge_send[slot, 1] = high
        edge_copy(slot, 0).start()
        edge_copy(slot, 1).start()

    def unpack(slot, r):
        low = edge_recv[slot, 1]
        high = edge_recv[slot, 0]
        low = pltpu.roll(low, (128 - 8 * r) % 128, 1) if r else low
        turn = (120 - 8 * r) % 128
        high = pltpu.roll(high, turn, 1) if turn else high
        return jnp.where(lane < 8, low, jnp.where(lane >= 120, high, 0.0))

    def set_split(r):
        high, low = split(out[0, r])
        x_high[r, :, 0:around] = high
        x_low[r, :, 0:around] = low

    for which in range(6, 11):
        loads[which].wait()
    turned = jnp.where(
        iota((taps, taps), 0) + iota((taps, taps), 1) == taps - 1, 1.0, 0.0
    ).astype(BF16)
    high, low = split(kernels_ref[...])
    rest = (kernels_ref[...] - high.astype(F32) - low.astype(F32)).astype(BF16)
    backward = dot(high, turned) + dot(low, turned) + dot(rest, turned)
    toeplitz[...] = jnp.zeros_like(toeplitz)
    constants[...] = jnp.zeros_like(constants)
    late = iota((1, taps), 1)
    for q in range(panels):
        row = backward[q : q + 1]
        for lag in range(ITERS):
            shifted = pltpu.roll(row, lag, 1) if lag else row
            toeplitz[8 * q + lag : 8 * q + lag + 1] = jnp.where(late >= lag, shifted, 0.0)
        constants[8 * q + 4 : 8 * q + 5] = jnp.full((1, slots), conduct_ref[q], F32)
        for k in range(ITERS - 1):
            constants[8 * q + 5 + k : 8 * q + 6 + k] = jnp.broadcast_to(
                kernels_ref[q : q + 1, k : k + 1], (1, slots)
            )
    loads[4].wait()
    ours = iota((8 * panels, slots), 0) >> 3

    lead, tail = split(toeplitz[...])
    both = jnp.concatenate([lead, tail], axis=0)

    def against(a, b):
        return lax.dot_general(a, b, (((1,), (1,)), ((), ())), preferred_element_type=F32)

    pairs = 2

    @pl.loop(0, n_wide // pairs)
    def _(block):
        size = pairs * slots
        high, low = split(history[pl.ds(pl.multiple_of(block * size, size), size)])
        full = against(both, high)
        full = full[: 8 * panels] + (full[8 * panels :] + against(lead, low))
        for k in range(pairs):
            o = block * pairs + k
            chosen = panel_ref[pl.ds(o, 1)] == ours
            terms = full[:, k * slots : (k + 1) * slots] + constants[...]
            terms = jnp.where(chosen, terms, 0.0)
            answer_send[o] = jnp.sum(terms.reshape(panels, 8, slots), axis=0)

    def answer_copy(k):
        peer = lax.rem(wide + k, n_wide)
        return pltpu.make_async_remote_copy(
            src_ref=answer_send.at[peer],
            dst_ref=answer_recv.at[wide],
            send_sem=answer_send_sem.at[k],
            recv_sem=answer_recv_sem.at[k],
            device_id={"wide": peer},
            device_id_type=MESH,
        )

    for k in range(1, n_wide):
        answer_copy(k).start()
    answer_recv[wide] = answer_send[wide]
    loads[0].wait()
    pack(0, 0)
    loads[3].wait()
    pack(3, ITERS)
    for r in range(layers):
        set_split(r)

    ring = around + 128
    gap = iota((ring, ring), 0) - iota((ring, ring), 1)
    gap = jnp.where(gap > ring // 2, gap - ring, jnp.where(gap < -(ring // 2), gap + ring, gap))
    bands[...] = band(gap).astype(BF16)
    size = blocks.shape[0]
    at_row, at_col = iota((size, size), 0), iota((size, size), 1)
    blocks[...] = jnp.where(
        (at_row // planes) == (at_col // planes), band(at_col - at_row), 0.0
    ).astype(BF16)

    shift = around.bit_length() - 1
    cells = cells_ref[...]
    own_row = cells >> shift
    side_row = beside_ref[...] >> shift
    stage[...] = jnp.zeros_like(stage)
    stage[0:n_wide] = own_row.astype(F32)
    stage[n_wide : 2 * n_wide] = (cells & (around - 1)).astype(F32)
    upright = jnp.transpose(stage[...])
    place = iota((slots, rows), 1).astype(F32)
    where = iota((slots, around), 1).astype(F32)
    level = iota((rows, slots), 0)
    for o in range(n_wide):
        span = slice(o * slots, (o + 1) * slots)
        pick[span] = jnp.where(place == upright[:, o : o + 1], 1.0, 0.0).astype(BF16)
        column[span] = jnp.where(
            where == upright[:, n_wide + o : n_wide + o + 1], 1.0, 0.0
        )
        spread[:, span] = (
            jnp.where(level == own_row[o : o + 1], 3.0, 0.0)
            + jnp.where(level == side_row[o : o + 1], 2.0, 0.0)
        ).astype(BF16)

    walls[...] = jnp.zeros_like(walls)
    live = jnp.where(iota((slots, n_wide), 0) < counts_ref[...], 1.0, 0.0)

    for k in range(1, n_wide):
        answer_copy(k).wait_recv()
    for o in range(n_wide):
        for m in range(8):
            stage[m * n_wide + o : m * n_wide + o + 1] = answer_recv[o, m : m + 1]
    upright = jnp.transpose(stage[...])
    for m in range(8):
        coefs[m] = upright[:, m * n_wide : (m + 1) * n_wide]

    edge_copy(ITERS, 0).wait_recv()
    edge_copy(ITERS, 1).wait_recv()
    for r in range(layers):
        around_side[r] = unpack(ITERS, r)
    for which in (1, 2, 5):
        loads[which].wait()

    group = size // planes
    fan = 4

    def pressure_at(step, r):
        if r < 0:
            return halo[step, 0, r + WIDE_HALO]
        if r >= layers:
            return halo[step, 1, r - layers]
        return out[0, r]

    def radial_at(r):
        if r < 0:
            return thin[0, r + THIN_HALO]
        if r >= layers:
            return thin[1, r - layers]
        return out[1, r]

    def differ(get, r):
        return (
            45.0 * (get(r + 1) - get(r - 1))
            - 9.0 * (get(r + 2) - get(r - 2))
            + (get(r + 3) - get(r - 3))
        )

    @pl.loop(0, ITERS)
    def _(step):
        for first in range(0, n_wide, fan):
            span = slice(first * slots, (first + fan) * slots)
            low = pick[span]
            found = dot(low, x_high[:, :, 0:around].reshape(rows, around)) + dot(
                low, x_low[:, :, 0:around].reshape(rows, around)
            )
            wall = jnp.sum(found * column[span], axis=1, keepdims=True)
            for o in range(fan):
                walls[0, :, first + o : first + o + 1] = wall[o * slots : (o + 1) * slots]
        wall = walls[0]
        velocity = coefs[4] * wall + coefs[step]
        for k in range(1, ITERS):
            velocity = velocity + coefs[4 + k] * walls[k]
        for k in range(ITERS - 1, 0, -1):
            walls[k] = walls[k - 1]
        flux = velocity * live
        for o in range(n_wide):
            span = slice(o * slots, (o + 1) * slots)
            high, low = split(flux[:, o : o + 1] * column[span])
            w_high[span] = high
            w_low[span] = low

        edge_copy(step, 0).wait_recv()
        edge_copy(step, 1).wait_recv()
        for r in range(layers):
            high, low = split(unpack(step, r))
            x_high[r, :, around:ring] = high
            x_low[r, :, around:ring] = low

        @pl.loop(0, layers // group)
        def _(chunk):
            part = pl.ds(chunk * group, group)
            span = pl.ds(pl.multiple_of(chunk * size, size), size)

            def flat(ref, width):
                return ref.reshape(size, width)

            high, low = flat(x_high[part], ring), flat(x_low[part], ring)
            along = dot(blocks[...], high[:, :around]) + dot(blocks[...], low[:, :around])
            axial = flat(out[2, part], around) - STEP * along
            out[2, part] = axial.reshape(group, planes, around)
            turn = dot(high, bands[...]) + dot(low, bands[...])
            inner = flat(out[3, part], around) - STEP * turn[:, :around]
            outer = flat(around_side[part], 128) - STEP * turn[:, around:]
            out[3, part] = inner.reshape(group, planes, around)
            around_side[part] = outer.reshape(group, planes, 128)
            high, low = split(axial)
            total = dot(blocks[...], high) + dot(blocks[...], low)
            for block, at in ((inner, slice(0, around)), (outer, slice(around, ring))):
                high, low = split(block)
                kept = bands[at, :around]
                total = total + (dot(high, kept) + dot(low, kept))
            added = dot(spread[span], w_high[...]) + dot(spread[span], w_low[...])
            base[part] = (
                flat(out[0, part], around)
                - (STEP * flat(stiff[part], around)) * total
                - 0.1 * added
            ).reshape(group, planes, around)

        get = functools.partial(pressure_at, step)
        for r in range(THIN_HALO, layers - THIN_HALO):
            out[1, r] = out[1, r] - STEP * differ(get, r)
        for side, there in sides:

            @pl.when(there)
            def _(side=side):
                radial_arrival(step, side).wait_recv()

                @pl.when(step == 0)
                def _():
                    thin_arrival(side).wait_recv()

        for r in range(THIN_HALO):
            out[1, r] = out[1, r] - STEP * differ(get, r)
            top = layers - 1 - r
            out[1, top] = out[1, top] - STEP * differ(get, top)
        for side, there in sides:

            @pl.when(there)
            def _(side=side):
                for k in range(THIN_HALO):
                    r = k - THIN_HALO if side == 0 else layers + k
                    thin[side, k] = thin[side, k] - STEP * differ(get, r)

                radial_copy(out, step, side).wait_send()

        def renew(r):
            out[0, r] = base[r] - (STEP * stiff[r]) * differ(radial_at, r)

        for r in range(WIDE_HALO):
            renew(r)

        @pl.when((step < ITERS - 1) & has_low)
        def _():
            radial_copy(out, step + 1, 0).start()

        for r in range(layers - WIDE_HALO, layers):
            renew(r)

        @pl.when((step < ITERS - 1) & has_high)
        def _():
            radial_copy(out, step + 1, 1).start()

        for r in range(WIDE_HALO, layers - WIDE_HALO):
            renew(r)

        @pl.when(step < ITERS - 1)
        def _():
            pack(0, step + 1)
            for r in range(layers):
                set_split(r)

    for side, there in sides:

        @pl.when(there)
        def _(side=side):
            thin_copy(side).wait_send()

    for slot in range(ITERS + 1):
        edge_copy(slot, 0).wait_send()
        edge_copy(slot, 1).wait_send()
    for k in range(1, n_wide):
        answer_copy(k).wait_send()


def shards(n_wide, n_narrow, *arrays):
    (state, stiffness, cells, besides, counts, history, panel, kernels, conductance) = arrays
    _, layers, planes, around = state.shape
    peers, slots = cells.shape[2:]
    taps = kernels.shape[1]
    panels = kernels.shape[0]
    rows, count, ring = layers * planes, peers * slots, around + 128
    group = max(1, min(layers, 256 // planes))
    any_space = pl.BlockSpec(memory_space=pltpu.HBM)
    vmem = pl.BlockSpec(memory_space=pltpu.VMEM)
    dma = pltpu.SemaphoreType.DMA
    scratch = [
        pltpu.VMEM((peers, slots), jnp.int32),
        pltpu.VMEM((peers, slots), jnp.int32),
        pltpu.VMEM((1, peers), jnp.int32),
        pltpu.VMEM((peers, slots), jnp.int32),
        pltpu.VMEM((panels, taps), F32),
        pltpu.VMEM((layers, planes, around), F32),
        pltpu.VMEM((count, taps), F32),
        pltpu.VMEM((ITERS, 2, WIDE_HALO, planes, around), F32),
        pltpu.VMEM((2, THIN_HALO, planes, around), F32),
        pltpu.VMEM((ITERS + 1, 2, planes, 128), F32),
        pltpu.VMEM((ITERS + 1, 2, planes, 128), F32),
        pltpu.VMEM((layers, planes, 128), F32),
        pltpu.VMEM((count, rows), BF16),
        pltpu.VMEM((rows, count), BF16),
        pltpu.VMEM((count, around), F32),
        pltpu.VMEM((layers, planes, ring), BF16),
        pltpu.VMEM((layers, planes, ring), BF16),
        pltpu.VMEM((count, around), BF16),
        pltpu.VMEM((count, around), BF16),
        pltpu.VMEM((layers, planes, around), F32),
        pltpu.VMEM((ring, ring), BF16),
        pltpu.VMEM((group * planes, group * planes), BF16),
        pltpu.VMEM((peers, 8, slots), F32),
        pltpu.VMEM((peers, 8, slots), F32),
        pltpu.VMEM((max(128, 8 * peers), slots), F32),
        pltpu.VMEM((8, slots, peers), F32),
        pltpu.VMEM((ITERS, slots, peers), F32),
        pltpu.VMEM((8 * panels, taps), F32),
        pltpu.VMEM((8 * panels, slots), F32),
        dma((11,)),
        dma((ITERS, 2)),
        dma((ITERS, 2)),
        dma((2,)),
        dma((2,)),
        dma((ITERS + 1, 2)),
        dma((ITERS + 1, 2)),
        dma((peers,)),
        dma((peers,)),
    ]
    return pl.pallas_call(
        functools.partial(kernel, n_wide, n_narrow),
        out_shape=jax.ShapeDtypeStruct(state.shape, F32),
        in_specs=[any_space] * 8 + [pl.BlockSpec(memory_space=pltpu.SMEM)],
        out_specs=vmem,
        scratch_shapes=scratch,
        compiler_params=pltpu.CompilerParams(
            collective_id=0, has_side_effects=True, vmem_limit_bytes=32 * 1024 * 1024
        ),
    )(
        *[
            pltpu.with_memory_space_constraint(array, pltpu.HBM)
            for array in (
                state,
                stiffness,
                cells.reshape(peers, slots),
                besides.reshape(peers, slots),
                counts.reshape(1, peers),
                history.reshape(count, taps),
                panel.reshape(peers, slots),
                kernels,
            )
        ],
        conductance,
    )


def solution(mesh):
    return jax.shard_map(
        functools.partial(shards, mesh.shape["wide"], mesh.shape["narrow"]),
        mesh=mesh,
        in_specs=(
            P(None, "narrow", None, "wide"),
            P("narrow", None, "wide"),
            P("narrow", "wide", None, None),
            P("narrow", "wide", None, None),
            P("narrow", "wide", None),
            P("narrow", "wide", None, None, None),
            P("narrow", "wide", None, None),
            P("wide", None),
            P("wide"),
        ),
        out_specs=P(None, "narrow", None, "wide"),
        check_vma=False,
    )
```

```python
import functools

import jax
import jax.numpy as jnp
from jax import lax
from jax.experimental import pallas as pl
from jax.experimental.pallas import tpu as pltpu
from jax.sharding import PartitionSpec as P

ITERS = 4
WIDE_HALO = 6
THIN_HALO = 3
STEP = 0.5 / 60.0
MESH = pl.DeviceIdType.MESH
F32 = jnp.float32
BF16 = jnp.bfloat16


def split(values):
    high = values.astype(BF16)
    return high, (values - high.astype(F32)).astype(BF16)


def dot(a, b):
    return jnp.dot(a, b, preferred_element_type=F32)


def band(offset):
    value = jnp.where(jnp.abs(offset) == 1, 45.0, 0.0)
    value = jnp.where(jnp.abs(offset) == 2, -9.0, value)
    value = jnp.where(jnp.abs(offset) == 3, 1.0, value)
    return jnp.where(offset < 0, -value, value)


def iota(shape, dim):
    return lax.broadcasted_iota(jnp.int32, shape, dim)


def kernel(
    n_wide,
    n_narrow,
    state,
    stiff_in,
    cells_in,
    beside_in,
    counts_in,
    history_in,
    panel_in,
    kernels_in,
    conduct_ref,
    out,
    cells_ref,
    beside_ref,
    counts_ref,
    panel_ref,
    kernels_ref,
    stiff,
    history,
    halo,
    thin,
    edge_send,
    edge_recv,
    around_side,
    pick,
    spread,
    column,
    x_high,
    x_low,
    w_high,
    w_low,
    base,
    bands,
    blocks,
    answer_send,
    answer_recv,
    stage,
    coefs,
    walls,
    toeplitz,
    constants,
    load_sem,
    radial_send,
    radial_recv,
    thin_send,
    thin_recv,
    edge_send_sem,
    edge_recv_sem,
    answer_send_sem,
    answer_recv_sem,
):
    wide = lax.axis_index("wide")
    narrow = lax.axis_index("narrow")
    layers, planes, around = out.shape[1:]
    rows, middle = layers * planes, planes // 2
    slots = panel_in.shape[1]
    panels, taps = kernels_in.shape
    left, right = lax.rem(wide + n_wide - 1, n_wide), lax.rem(wide + 1, n_wide)
    has_low, has_high = narrow > 0, narrow < n_narrow - 1

    loads = [
        pltpu.make_async_copy(state.at[k], out.at[k], load_sem.at[k]) for k in range(4)
    ]
    loads.append(pltpu.make_async_copy(history_in, history, load_sem.at[4]))
    loads.append(pltpu.make_async_copy(stiff_in, stiff, load_sem.at[5]))
    small = (
        (cells_in, cells_ref),
        (beside_in, beside_ref),
        (counts_in, counts_ref),
        (panel_in, panel_ref),
        (kernels_in, kernels_ref),
    )
    for k, (source, target) in enumerate(small):
        loads.append(pltpu.make_async_copy(source, target, load_sem.at[6 + k]))
    for which in (6, 7, 8, 9, 10, 0, 4, 3, 1, 2, 5):
        loads[which].start()

    barrier = pltpu.get_barrier_semaphore()
    for k in range(1, n_wide):
        peer = lax.rem(wide + k, n_wide)
        pl.semaphore_signal(barrier, inc=1, device_id={"wide": peer}, device_id_type=MESH)

    @pl.when(has_low)
    def _():
        pl.semaphore_signal(
            barrier, inc=1, device_id={"narrow": narrow - 1}, device_id_type=MESH
        )

    @pl.when(has_high)
    def _():
        pl.semaphore_signal(
            barrier, inc=1, device_id={"narrow": narrow + 1}, device_id_type=MESH
        )

    @pl.when(jnp.logical_not(has_low))
    def _():
        halo[:, 0] = jnp.zeros(halo.shape[:1] + halo.shape[2:], F32)
        thin[0] = jnp.zeros(thin.shape[1:], F32)

    @pl.when(jnp.logical_not(has_high))
    def _():
        halo[:, 1] = jnp.zeros(halo.shape[:1] + halo.shape[2:], F32)
        thin[1] = jnp.zeros(thin.shape[1:], F32)

    beside = jnp.where(has_low, 1, 0) + jnp.where(has_high, 1, 0)
    pl.semaphore_wait(barrier, n_wide - 1 + beside)

    def radial_copy(source, step, side, half, peer=None):
        if peer is None:
            peer = narrow - 1 if side == 0 else narrow + 1
        first = 0 if side == 0 else layers - WIDE_HALO
        return pltpu.make_async_remote_copy(
            src_ref=source.at[0, pl.ds(first, WIDE_HALO), pl.ds(half * middle, middle)],
            dst_ref=halo.at[step, 1 - side, :, pl.ds(half * middle, middle)],
            send_sem=radial_send.at[step, side, half],
            recv_sem=radial_recv.at[step, 1 - side, half],
            device_id={"narrow": peer},
            device_id_type=MESH,
        )

    def thin_copy(side, peer=None):
        if peer is None:
            peer = narrow - 1 if side == 0 else narrow + 1
        first = 0 if side == 0 else layers - THIN_HALO
        return pltpu.make_async_remote_copy(
            src_ref=state.at[1, pl.ds(first, THIN_HALO)],
            dst_ref=thin.at[1 - side],
            send_sem=thin_send.at[side],
            recv_sem=thin_recv.at[1 - side],
            device_id={"narrow": peer},
            device_id_type=MESH,
        )

    def radial_arrival(step, side, half):
        return radial_copy(out, step, 1 - side, half, narrow - 1 if side == 0 else narrow + 1)

    def thin_arrival(side):
        return thin_copy(1 - side, narrow - 1 if side == 0 else narrow + 1)

    def edge_copy(slot, side):
        return pltpu.make_async_remote_copy(
            src_ref=edge_send.at[slot, side],
            dst_ref=edge_recv.at[slot, 1 - side],
            send_sem=edge_send_sem.at[slot, side],
            recv_sem=edge_recv_sem.at[slot, 1 - side],
            device_id={"wide": left if side == 0 else right},
            device_id_type=MESH,
        )

    sides = ((0, has_low), (1, has_high))
    for side, there in sides:

        @pl.when(there)
        def _(side=side):
            radial_copy(state, 0, side, 0).start()
            thin_copy(side).start()
            radial_copy(state, 0, side, 1).start()

    lane = iota((planes, 128), 1)

    def pack(field, slot):
        low = jnp.zeros((planes, 128), F32)
        high = jnp.zeros((planes, 128), F32)
        for r in range(layers):
            here = (lane >= 8 * r) & (lane < 8 * r + 8)
            first = out[field, r, :, 0:128]
            last = out[field, r, :, around - 128 : around]
            low = jnp.where(here, pltpu.roll(first, 8 * r, 1) if r else first, low)
            high = jnp.where(here, pltpu.roll(last, (8 * r + 8) % 128, 1), high)
        edge_send[slot, 0] = low
        edge_send[slot, 1] = high
        edge_copy(slot, 0).start()
        edge_copy(slot, 1).start()

    def unpack(slot, r):
        low = edge_recv[slot, 1]
        high = edge_recv[slot, 0]
        low = pltpu.roll(low, (128 - 8 * r) % 128, 1) if r else low
        turn = (120 - 8 * r) % 128
        high = pltpu.roll(high, turn, 1) if turn else high
        return jnp.where(lane < 8, low, jnp.where(lane >= 120, high, 0.0))

    def set_split(r):
        high, low = split(out[0, r])
        x_high[r, :, 0:around] = high
        x_low[r, :, 0:around] = low

    for which in range(6, 11):
        loads[which].wait()
    turned = jnp.where(
        iota((taps, taps), 0) + iota((taps, taps), 1) == taps - 1, 1.0, 0.0
    ).astype(BF16)
    high, low = split(kernels_ref[...])
    rest = (kernels_ref[...] - high.astype(F32) - low.astype(F32)).astype(BF16)
    backward = dot(high, turned) + dot(low, turned) + dot(rest, turned)
    toeplitz[...] = jnp.zeros_like(toeplitz)
    constants[...] = jnp.zeros_like(constants)
    late = iota((1, taps), 1)
    for q in range(panels):
        row = backward[q : q + 1]
        for lag in range(ITERS):
            shifted = pltpu.roll(row, lag, 1) if lag else row
            toeplitz[8 * q + lag : 8 * q + lag + 1] = jnp.where(late >= lag, shifted, 0.0)
        constants[8 * q + 4 : 8 * q + 5] = jnp.full((1, slots), conduct_ref[q], F32)
        for k in range(ITERS - 1):
            constants[8 * q + 5 + k : 8 * q + 6 + k] = jnp.broadcast_to(
                kernels_ref[q : q + 1, k : k + 1], (1, slots)
            )
    loads[4].wait()
    ours = iota((8 * panels, slots), 0) >> 3

    lead, tail = split(toeplitz[...])
    both = jnp.concatenate([lead, tail], axis=0)

    def against(a, b):
        return lax.dot_general(a, b, (((1,), (1,)), ((), ())), preferred_element_type=F32)

    pairs = 2

    @pl.loop(0, n_wide // pairs)
    def _(block):
        size = pairs * slots
        high, low = split(history[pl.ds(pl.multiple_of(block * size, size), size)])
        full = against(both, high)
        full = full[: 8 * panels] + (full[8 * panels :] + against(lead, low))
        for k in range(pairs):
            o = block * pairs + k
            chosen = panel_ref[pl.ds(o, 1)] == ours
            terms = full[:, k * slots : (k + 1) * slots] + constants[...]
            terms = jnp.where(chosen, terms, 0.0)
            answer_send[o] = jnp.sum(terms.reshape(panels, 8, slots), axis=0)

    def answer_copy(k):
        peer = lax.rem(wide + k, n_wide)
        return pltpu.make_async_remote_copy(
            src_ref=answer_send.at[peer],
            dst_ref=answer_recv.at[wide],
            send_sem=answer_send_sem.at[k],
            recv_sem=answer_recv_sem.at[k],
            device_id={"wide": peer},
            device_id_type=MESH,
        )

    for k in range(1, n_wide):
        answer_copy(k).start()
    answer_recv[wide] = answer_send[wide]
    loads[0].wait()
    pack(0, 0)
    loads[3].wait()
    pack(3, ITERS)
    for r in range(layers):
        set_split(r)

    ring = around + 128
    gap = iota((ring, ring), 0) - iota((ring, ring), 1)
    gap = jnp.where(gap > ring // 2, gap - ring, jnp.where(gap < -(ring // 2), gap + ring, gap))
    bands[...] = band(gap).astype(BF16)
    size = blocks.shape[0]
    at_row, at_col = iota((size, size), 0), iota((size, size), 1)
    blocks[...] = jnp.where(
        (at_row // planes) == (at_col // planes), band(at_col - at_row), 0.0
    ).astype(BF16)

    shift = around.bit_length() - 1
    cells = cells_ref[...]
    own_row = cells >> shift
    side_row = beside_ref[...] >> shift
    stage[...] = jnp.zeros_like(stage)
    stage[0:n_wide] = own_row.astype(F32)
    stage[n_wide : 2 * n_wide] = (cells & (around - 1)).astype(F32)
    upright = jnp.transpose(stage[...])
    place = iota((slots, rows), 1).astype(F32)
    where = iota((slots, around), 1).astype(F32)
    level = iota((rows, slots), 0)
    for o in range(n_wide):
        span = slice(o * slots, (o + 1) * slots)
        pick[span] = jnp.where(place == upright[:, o : o + 1], 1.0, 0.0).astype(BF16)
        column[span] = jnp.where(
            where == upright[:, n_wide + o : n_wide + o + 1], 1.0, 0.0
        )
        spread[:, span] = (
            jnp.where(level == own_row[o : o + 1], 3.0, 0.0)
            + jnp.where(level == side_row[o : o + 1], 2.0, 0.0)
        ).astype(BF16)

    walls[...] = jnp.zeros_like(walls)
    live = jnp.where(iota((slots, n_wide), 0) < counts_ref[...], 1.0, 0.0)

    for k in range(1, n_wide):
        answer_copy(k).wait_recv()
    for o in range(n_wide):
        for m in range(8):
            stage[m * n_wide + o : m * n_wide + o + 1] = answer_recv[o, m : m + 1]
    upright = jnp.transpose(stage[...])
    for m in range(8):
        coefs[m] = upright[:, m * n_wide : (m + 1) * n_wide]

    edge_copy(ITERS, 0).wait_recv()
    edge_copy(ITERS, 1).wait_recv()
    for r in range(layers):
        around_side[r] = unpack(ITERS, r)
    for which in (1, 2, 5):
        loads[which].wait()

    group = size // planes
    fan = 4

    def pressure_at(step, span, r):
        if r < 0:
            return halo[step, 0, r + WIDE_HALO, span]
        if r >= layers:
            return halo[step, 1, r - layers, span]
        return out[0, r, span]

    def radial_at(span, r):
        if r < 0:
            return thin[0, r + THIN_HALO, span]
        if r >= layers:
            return thin[1, r - layers, span]
        return out[1, r, span]

    def set_radial(span, r, values):
        if r < 0:
            thin[0, r + THIN_HALO, span] = values
        elif r >= layers:
            thin[1, r - layers, span] = values
        else:
            out[1, r, span] = values

    def differences(get, first, last):
        held = {r: get(r) for r in range(first - 3, last + 3)}
        return {
            r: (45.0 * STEP) * (held[r + 1] - held[r - 1])
            - (9.0 * STEP) * (held[r + 2] - held[r - 2])
            + STEP * (held[r + 3] - held[r - 3])
            for r in range(first, last)
        }

    def sweep(half):
        first, last = (0, planes) if half is None else (half * middle, (half + 1) * middle)
        return lambda body: pl.loop(first // 16, last // 16)(
            lambda k: body(pl.ds(pl.multiple_of(k * 16, 16), 16))
        )

    def push_radial(step, first, last, half=None):
        @sweep(half)
        def _(span):
            slopes = differences(functools.partial(pressure_at, step, span), first, last)
            for r, slope in slopes.items():
                set_radial(span, r, radial_at(span, r) - slope)

    def renew(first, last, half=None):
        @sweep(half)
        def _(span):
            slopes = differences(functools.partial(radial_at, span), first, last)
            for r, slope in slopes.items():
                fresh = base[r, span] - stiff[r, span] * slope
                out[0, r, span] = fresh
                high, low = split(fresh)
                x_high[r, span, 0:around] = high
                x_low[r, span, 0:around] = low

    @pl.loop(0, ITERS)
    def _(step):
        for first in range(0, n_wide, fan):
            span = slice(first * slots, (first + fan) * slots)
            low = pick[span]
            found = dot(low, x_high[:, :, 0:around].reshape(rows, around)) + dot(
                low, x_low[:, :, 0:around].reshape(rows, around)
            )
            wall = jnp.sum(found * column[span], axis=1, keepdims=True)
            for o in range(fan):
                walls[0, :, first + o : first + o + 1] = wall[o * slots : (o + 1) * slots]
        wall = walls[0]
        velocity = coefs[4] * wall + coefs[step]
        for k in range(1, ITERS):
            velocity = velocity + coefs[4 + k] * walls[k]
        for k in range(ITERS - 1, 0, -1):
            walls[k] = walls[k - 1]
        flux = velocity * live
        for o in range(n_wide):
            span = slice(o * slots, (o + 1) * slots)
            high, low = split(flux[:, o : o + 1] * column[span])
            w_high[span] = high
            w_low[span] = low

        push_radial(step, THIN_HALO, layers - THIN_HALO)
        edge_copy(step, 0).wait_recv()
        edge_copy(step, 1).wait_recv()
        for r in range(layers):
            high, low = split(unpack(step, r))
            x_high[r, :, around:ring] = high
            x_low[r, :, around:ring] = low

        @pl.loop(0, layers // group)
        def _(chunk):
            part = pl.ds(chunk * group, group)
            span = pl.ds(pl.multiple_of(chunk * size, size), size)

            def flat(ref, width):
                return ref.reshape(size, width)

            high, low = flat(x_high[part], ring), flat(x_low[part], ring)
            along = dot(blocks[...], high[:, :around]) + dot(blocks[...], low[:, :around])
            axial = flat(out[2, part], around) - STEP * along
            out[2, part] = axial.reshape(group, planes, around)
            turn = dot(jnp.concatenate([high, low], axis=0), bands[...])
            turn = turn[:size] + turn[size:]
            inner = flat(out[3, part], around) - STEP * turn[:, :around]
            outer = flat(around_side[part], 128) - STEP * turn[:, around:]
            out[3, part] = inner.reshape(group, planes, around)
            around_side[part] = outer.reshape(group, planes, 128)
            high, low = split(axial)
            total = dot(blocks[...], high) + dot(blocks[...], low)
            for block, at in ((inner, slice(0, around)), (outer, slice(around, ring))):
                high, low = split(block)
                kept = bands[at, :around]
                both = dot(jnp.concatenate([high, low], axis=0), kept)
                total = total + (both[:size] + both[size:])
            added = dot(spread[span], w_high[...]) + dot(spread[span], w_low[...])
            base[part] = (
                flat(out[0, part], around)
                - STEP * flat(stiff[part], around) * total
                - 0.1 * added
            ).reshape(group, planes, around)

        for half in range(2):
            for side, there in sides:
                inside, end = (0, THIN_HALO) if side == 0 else (layers - THIN_HALO, layers)

                @pl.when(there)
                def _(side=side, half=half):
                    radial_arrival(step, side, half).wait_recv()
                    if half == 0:

                        @pl.when(step == 0)
                        def _():
                            thin_arrival(side).wait_recv()

                    if side == 0:
                        push_radial(step, -THIN_HALO, THIN_HALO, half)
                    else:
                        push_radial(step, layers - THIN_HALO, layers + THIN_HALO, half)
                    radial_copy(out, step, side, half).wait_send()

                @pl.when(jnp.logical_not(there))
                def _(inside=inside, end=end, half=half):
                    push_radial(step, inside, end, half)

            for side, there in sides:
                if side == 0:
                    renew(0, WIDE_HALO, half)
                else:
                    renew(layers - WIDE_HALO, layers, half)

                @pl.when((step < ITERS - 1) & there)
                def _(side=side, half=half):
                    radial_copy(out, step + 1, side, half).start()

        renew(WIDE_HALO, layers - WIDE_HALO)

        @pl.when(step < ITERS - 1)
        def _():
            pack(0, step + 1)

    for side, there in sides:

        @pl.when(there)
        def _(side=side):
            thin_copy(side).wait_send()

    for slot in range(ITERS + 1):
        edge_copy(slot, 0).wait_send()
        edge_copy(slot, 1).wait_send()
    for k in range(1, n_wide):
        answer_copy(k).wait_send()


def shards(n_wide, n_narrow, *arrays):
    (state, stiffness, cells, besides, counts, history, panel, kernels, conductance) = arrays
    _, layers, planes, around = state.shape
    peers, slots = cells.shape[2:]
    taps = kernels.shape[1]
    panels = kernels.shape[0]
    rows, count, ring = layers * planes, peers * slots, around + 128
    group = max(1, min(layers, 256 // planes))
    any_space = pl.BlockSpec(memory_space=pltpu.HBM)
    vmem = pl.BlockSpec(memory_space=pltpu.VMEM)
    dma = pltpu.SemaphoreType.DMA
    scratch = [
        pltpu.VMEM((peers, slots), jnp.int32),
        pltpu.VMEM((peers, slots), jnp.int32),
        pltpu.VMEM((1, peers), jnp.int32),
        pltpu.VMEM((peers, slots), jnp.int32),
        pltpu.VMEM((panels, taps), F32),
        pltpu.VMEM((layers, planes, around), F32),
        pltpu.VMEM((count, taps), F32),
        pltpu.VMEM((ITERS, 2, WIDE_HALO, planes, around), F32),
        pltpu.VMEM((2, THIN_HALO, planes, around), F32),
        pltpu.VMEM((ITERS + 1, 2, planes, 128), F32),
        pltpu.VMEM((ITERS + 1, 2, planes, 128), F32),
        pltpu.VMEM((layers, planes, 128), F32),
        pltpu.VMEM((count, rows), BF16),
        pltpu.VMEM((rows, count), BF16),
        pltpu.VMEM((count, around), F32),
        pltpu.VMEM((layers, planes, ring), BF16),
        pltpu.VMEM((layers, planes, ring), BF16),
        pltpu.VMEM((count, around), BF16),
        pltpu.VMEM((count, around), BF16),
        pltpu.VMEM((layers, planes, around), F32),
        pltpu.VMEM((ring, ring), BF16),
        pltpu.VMEM((group * planes, group * planes), BF16),
        pltpu.VMEM((peers, 8, slots), F32),
        pltpu.VMEM((peers, 8, slots), F32),
        pltpu.VMEM((max(128, 8 * peers), slots), F32),
        pltpu.VMEM((8, slots, peers), F32),
        pltpu.VMEM((ITERS, slots, peers), F32),
        pltpu.VMEM((8 * panels, taps), F32),
        pltpu.VMEM((8 * panels, slots), F32),
        dma((11,)),
        dma((ITERS, 2, 2)),
        dma((ITERS, 2, 2)),
        dma((2,)),
        dma((2,)),
        dma((ITERS + 1, 2)),
        dma((ITERS + 1, 2)),
        dma((peers,)),
        dma((peers,)),
    ]
    return pl.pallas_call(
        functools.partial(kernel, n_wide, n_narrow),
        out_shape=jax.ShapeDtypeStruct(state.shape, F32),
        in_specs=[any_space] * 8 + [pl.BlockSpec(memory_space=pltpu.SMEM)],
        out_specs=vmem,
        scratch_shapes=scratch,
        compiler_params=pltpu.CompilerParams(
            collective_id=0, has_side_effects=True, vmem_limit_bytes=32 * 1024 * 1024
        ),
    )(
        *[
            pltpu.with_memory_space_constraint(array, pltpu.HBM)
            for array in (
                state,
                stiffness,
                cells.reshape(peers, slots),
                besides.reshape(peers, slots),
                counts.reshape(1, peers),
                history.reshape(count, taps),
                panel.reshape(peers, slots),
                kernels,
            )
        ],
        conductance,
    )


def solution(mesh):
    return jax.shard_map(
        functools.partial(shards, mesh.shape["wide"], mesh.shape["narrow"]),
        mesh=mesh,
        in_specs=(
            P(None, "narrow", None, "wide"),
            P("narrow", None, "wide"),
            P("narrow", "wide", None, None),
            P("narrow", "wide", None, None),
            P("narrow", "wide", None),
            P("narrow", "wide", None, None, None),
            P("narrow", "wide", None, None),
            P("wide", None),
            P("wide"),
        ),
        out_specs=P(None, "narrow", None, "wide"),
        check_vma=False,
    )
```
